256 devices in a mesh: blk: 32 (over z, x_lo, core), inner: 8 (over y, x_hi).
Axes of the slice: x: 4 (x_hi: 2, x_lo: 2; x = x_hi * 2 + x_lo), y: 4, z: 8, core: 2. Of those that a mesh axis runs over, the one named last changes fastest.
Arguments:
- echo_vectors: bfloat16 [32768, 768], P(('blk', 'inner')), may hold values from -9 to 9
- footage_vectors: bfloat16 [32768, 768], P(('blk', 'inner')), may hold values from -9 to 9
- match_numbers: int32 [32768], P(('blk', 'inner')), may hold values from 0 to 8191, as said below
- sharpness_factor: float32 [1], replicated, may hold values from 30 to 50
- score_offset: float32 [1], replicated, may hold values from -11 to -9
Outputs:
- grad_image: bfloat16 [32768, 768], P(('blk', 'inner'))
- grad_text: bfloat16 [32768, 768], P(('blk', 'inner'))
- loss: float32 [1], replicated
The draws below stay inside these ranges and needn't reach their ends.
Inputs may be any that keep to these rules, and one draw needn't show every extreme that they name: `match_numbers`: at most 8192 distinct ids; clips that share an id form positive pairs.
All inputs are finite; a program needn't handle non-finite values.
Results may differ from the reference program's by a relative error of at most 0.013.
Values may be sent and summed in bfloat16 or wider, within the bound.
A program may use at most 64 MiB of HBM per device.

```python
import math
import jax
import jax.numpy as jnp
from jax import lax

D = 768
BATCH = 32768


def shared_ids(key):
    labels = jax.random.randint(jax.random.fold_in(key, 101), (BATCH,), 0, BATCH // 4)
    labels = labels.at[0].set(0)
    labels = labels.at[BATCH - 1].set(BATCH // 4 - 1)
    return labels.astype(jnp.int32)


def shared_rows(key):
    labels = shared_ids(key)
    protos = jnp.clip(jax.random.normal(jax.random.fold_in(key, 102), (BATCH // 4, D), jnp.float32), -4.0, 4.0)
    return protos[labels]


def mix_rows(key, aligned, noise, scale_lo, scale_hi):
    align_weight = jax.random.uniform(jax.random.fold_in(key, 5), (BATCH, 1), jnp.float32, 0.3, 1.2)
    log_scale = jax.random.uniform(jax.random.fold_in(key, 6), (BATCH, 1), jnp.float32, math.log(scale_lo), math.log(scale_hi))
    rows = jnp.exp(log_scale) * (align_weight * aligned + noise)
    return rows.astype(jnp.bfloat16)


def draw_match_numbers(key, part):
    return shared_ids(key)


def draw_echo_vectors(key, part):
    aligned = shared_rows(key)
    key = jax.random.fold_in(key, 1)
    noise = jnp.clip(jax.random.normal(jax.random.fold_in(key, 7), (BATCH, D), jnp.float32), -4.0, 4.0)
    return mix_rows(key, aligned, noise, 0.1, 1.0)


def draw_footage_vectors(key, part):
    aligned = shared_rows(key)
    key = jax.random.fold_in(key, 2)
    noise = jnp.clip(jax.random.normal(jax.random.fold_in(key, 7), (BATCH, D), jnp.float32), -4.0, 4.0)
    return mix_rows(key, aligned, noise, 0.1, 1.0)


def setup_inputs(seed: int = 0) -> dict:
    key_of = jax.random.split(jax.random.key(seed), 6)
    echo_vectors = draw_echo_vectors(jax.random.fold_in(key_of[5], 71), 0)
    footage_vectors = draw_footage_vectors(jax.random.fold_in(key_of[5], 71), 0)
    match_numbers = draw_match_numbers(jax.random.fold_in(key_of[5], 71), 0)
    sharpness_factor = jnp.clip(jnp.exp(jax.random.uniform(key_of[3], (1,), jnp.float32, math.log(30.0), math.log(50.0))), 30.0, 50.0)
    score_offset = jnp.clip(jax.random.uniform(key_of[4], (1,), jnp.float32, -11.0, -9.0), -11.0, -9.0)
    return dict(echo_vectors=echo_vectors, footage_vectors=footage_vectors, match_numbers=match_numbers, sharpness_factor=sharpness_factor, score_offset=score_offset)


def normalize(raw):
    values = raw.astype(jnp.float32)
    row_norm = jnp.sqrt(lax.optimization_barrier(jnp.sum(values * values, axis=-1, keepdims=True)) + 1e-06)
    return (values / row_norm, row_norm)

def unit_back(unit_f32, row_norm, unit_grad):
    inner_prod = lax.optimization_barrier(jnp.sum(unit_f32 * unit_grad, axis=-1, keepdims=True))
    return ((unit_grad - unit_f32 * inner_prod) / row_norm).astype(jnp.bfloat16)

def reference(echo_vectors, footage_vectors, match_numbers, sharpness_factor, score_offset):
    image_f32, image_norm = normalize(echo_vectors)
    text_f32, text_norm = normalize(footage_vectors)
    image_unit = image_f32.astype(jnp.bfloat16)
    text_unit = text_f32.astype(jnp.bfloat16)
    score_factor = sharpness_factor[0]
    logit_bias = score_offset[0]
    block_rows = math.gcd(BATCH, 512)
    count = BATCH // block_rows
    picture_slices = image_unit.reshape(count, block_rows, D)
    id_blocks = match_numbers.reshape(count, block_rows)

    def visit(loop_state, inputs):
        video_embedding_gradient, loss_sum = loop_state
        image_rows, image_ids = inputs
        logits = score_factor * lax.dot_general(image_rows, text_unit, (((1,), (1,)), ((), ())), preferred_element_type=jnp.float32) + logit_bias
        label_sign = jnp.where(image_ids[:, None] == match_numbers[None, :], 1.0, -1.0).astype(jnp.float32)
        loss_sum = loss_sum + jnp.sum(jax.nn.log_sigmoid(label_sign * logits))
        weights = (-label_sign * jax.nn.sigmoid(-label_sign * logits) * score_factor).astype(jnp.bfloat16)
        image_part = jnp.dot(weights, text_unit, preferred_element_type=jnp.float32)
        video_embedding_gradient = video_embedding_gradient + lax.dot_general(weights, image_rows, (((0,), (0,)), ((), ())), preferred_element_type=jnp.float32)
        return ((video_embedding_gradient, loss_sum), image_part)
    start = (jnp.zeros((BATCH, D), jnp.float32), jnp.zeros((), jnp.float32))
    (video_embedding_gradient, loss_sum), image_parts = lax.scan(visit, start, (picture_slices, id_blocks))
    image_grad = image_parts.reshape(BATCH, D)
    grad_image = unit_back(image_f32, image_norm, image_grad)
    grad_text = unit_back(text_f32, text_norm, video_embedding_gradient)
    loss = (-loss_sum / BATCH).reshape(1)
    return (grad_image, grad_text, loss)
```

```python
import functools
import math

import jax
import jax.numpy as jnp
from jax import lax
from jax.experimental import pallas as pl
from jax.experimental.pallas import tpu as pltpu
from jax.sharding import PartitionSpec as P

ROWS, D = 128, 768
TILES = D // 128
BLOCK = D + 16
SLOTS = 16
N = SLOTS * ROWS
BATCH = 32768
MESH = pl.DeviceIdType.MESH

WHOLE, A, B = (0, BLOCK), (0, 384), (384, BLOCK)
A0, A1, B0, B1 = (0, 192), (192, 384), (384, 576), (576, BLOCK)

PLACES = [
    (0, 0), (1, 0), (3, 0), (0, 1), (0, 3),
    (2, 0), (0, 2), (1, 1), (1, 3), (3, 1), (3, 3),
    (2, 1), (2, 3), (1, 2), (3, 2), (2, 2),
]
ISLOT = {place: slot for slot, place in enumerate(PLACES)}
STEP = {"+x": (1, 0), "-x": (3, 0), "+y": (0, 1), "-y": (0, 3)}
BACK = {"+x": "-x", "-x": "+x", "+y": "-y", "-y": "+y", "+z": "-z", "-z": "+z"}
IMG = [
    [((0, 0), WHOLE, d) for d in ("+x", "-x", "+y", "-y")],
    [
        ((0, 1), B, "+x"), ((0, 1), B, "-x"), ((1, 0), A, "+y"), ((1, 0), A, "-y"),
        ((0, 3), B, "+x"), ((0, 3), B, "-x"), ((3, 0), A, "+y"), ((3, 0), A, "-y"),
        ((3, 0), A, "+x"), ((1, 0), B, "-x"), ((0, 3), A, "+y"), ((0, 1), B, "-y"),
    ],
    [
        ((0, 2), B, "+x"), ((0, 2), B, "-x"), ((2, 0), A, "+y"), ((2, 0), A, "-y"),
        ((3, 1), B0, "+x"), ((1, 1), B1, "-x"), ((1, 3), A0, "+y"), ((1, 1), A1, "-y"),
        ((3, 3), B0, "+x"), ((1, 3), B1, "-x"), ((3, 3), A0, "+y"), ((3, 1), A1, "-y"),
    ],
    [((3, 2), B0, "+x"), ((1, 2), B1, "-x"), ((2, 3), A0, "+y"), ((2, 1), A1, "-y")],
]
DZ = [0, 1, 7, 2, 6, 3, 5, 4]
TPLACE = {dz: k for k, dz in enumerate(DZ)}
TXT = [
    [(0, WHOLE, "+z"), (0, WHOLE, "-z")],
    [(7, WHOLE, "+z"), (1, WHOLE, "-z")],
    [(6, WHOLE, "+z"), (2, WHOLE, "-z")],
    [(5, A, "+z"), (3, B, "-z")],
]
FRESH = [[0], [1, 7], [2, 6], [3, 5], [4]]


def img_to(place, direction):
    sx, sy = STEP[direction]
    return ((place[0] - sx) % 4, (place[1] - sy) % 4)


def txt_to(dz, direction):
    return (dz - 1) % 8 if direction == "+z" else (dz + 1) % 8


def numbered(rounds, to, slot_of):
    gather, scatter, count, land = [], [], 0, 0
    for moves in rounds:
        out, back = [], []
        for place, (lo, hi), direction in moves:
            there = to(place, direction)
            out.append((count, slot_of[place], slot_of[there], lo, hi, direction))
            top = min(hi, D)
            back.append((count, slot_of[there], slot_of[place], lo, top, BACK[direction], land))
            land += top - lo
            count += 1
        gather.append(out)
        scatter.append(back)
    return gather, scatter, count, land


IMG_OUT, IMG_BACK, IMG_N, IMG_LAND = numbered(IMG, img_to, ISLOT)
TXT_OUT, TXT_BACK, TXT_N, TXT_LAND = numbered(TXT, txt_to, TPLACE)


def spans(lo, hi):
    parts = []
    while lo < hi:
        tile = lo // 128
        end = min(hi, (tile + 1) * 128)
        parts.append((tile, lo - tile * 128, end - tile * 128))
        lo = end
    return parts


def kernel(
    echo_ref, footage_ref, ids_ref, sharp_ref, offset_ref,
    gimg_ref, gtxt_ref, loss_ref,
    irx, trx, img, txt, idi, idt, gi, gt,
    isend, iland, tsend, tland, ssend, sland,
    total, lc, lx, ly, lz,
    ig_s, ig_r, tg_s, tg_r, sg_s, sg_r,
    is_s, is_r, ts_s, ts_r, ss_s, ss_r, l_s, l_r,
):
    blk, inner = lax.axis_index("blk"), lax.axis_index("inner")
    core = lax.rem(blk, 2)
    z = lax.div(blk, 4)
    x = lax.rem(inner, 2) * 2 + lax.rem(lax.div(blk, 2), 2)
    y = lax.div(inner, 2)

    def at(z, x, y, core):
        return {
            "blk": z * 4 + lax.rem(x, 2) * 2 + core,
            "inner": y * 2 + lax.div(x, 2),
        }

    xs = [at(z, lax.rem(x + k, 4), y, core) for k in range(4)]
    ys = [at(z, x, lax.rem(y + k, 4), core) for k in range(4)]
    zs = [at(lax.rem(z + k, 8), x, y, core) for k in range(8)]
    sib = at(z, x, y, 1 - core)
    near = {"+x": xs[1], "-x": xs[3], "+y": ys[1], "-y": ys[3], "+z": zs[1], "-z": zs[7]}

    barrier = pltpu.get_barrier_semaphore()
    partners = xs[1:] + ys[1:] + zs[1:] + [sib]
    for device in partners:
        pl.semaphore_signal(barrier, inc=1, device_id=device, device_id_type=MESH)

    def unit32(ref):
        values = ref[...].astype(jnp.float32)
        norm = jnp.sqrt(jnp.sum(values * values, axis=-1, keepdims=True) + 1e-06)
        return values / norm, norm

    ids = ids_ref[...]
    row = lax.broadcasted_iota(jnp.int32, (16, 128), 0)
    high = jnp.broadcast_to((ids >> 6).astype(jnp.float32), (16, 128))
    low = jnp.broadcast_to((ids & 63).astype(jnp.float32), (16, 128))
    id_rows = jnp.where(row == 0, high, jnp.where(row == 1, low, 0.0)).astype(jnp.bfloat16)
    for ref, slots in ((echo_ref, irx), (footage_ref, trx)):
        unit = unit32(ref)[0].astype(jnp.bfloat16)
        for c in range(TILES):
            slots[pl.ds(c * 128, 128), :] = unit[:, c * 128 : (c + 1) * 128]
        slots[pl.ds(D, 16), :] = id_rows

    pl.semaphore_wait(barrier, len(partners))

    def remote(src, dst, send, recv, device):
        return pltpu.make_async_remote_copy(
            src_ref=src, dst_ref=dst, send_sem=send, recv_sem=recv,
            device_id=device, device_id_type=MESH,
        )

    def img_copy(move):
        k, slot, there, lo, hi, direction = move
        return remote(
            irx.at[pl.ds(slot * BLOCK + lo, hi - lo)], irx.at[pl.ds(there * BLOCK + lo, hi - lo)],
            ig_s.at[k], ig_r.at[k], near[direction],
        )

    def txt_copy(move):
        k, slot, there, lo, hi, direction = move
        return remote(
            trx.at[pl.ds(slot * BLOCK + lo, hi - lo)], trx.at[pl.ds(there * BLOCK + lo, hi - lo)],
            tg_s.at[k], tg_r.at[k], near[direction],
        )

    def sib_copy(k):
        return remote(
            trx.at[pl.ds(k * BLOCK, BLOCK)], trx.at[pl.ds((8 + k) * BLOCK, BLOCK)],
            sg_s.at[k], sg_r.at[k], sib,
        )

    def img_start(r):
        for move in IMG_OUT[r]:
            img_copy(move).start()

    def img_wait(r):
        for move in IMG_OUT[r]:
            img_copy(move).wait_recv()

    def txt_start(r):
        if r < 4:
            for move in TXT_OUT[r]:
                txt_copy(move).start()
        for dz in FRESH[r]:
            sib_copy(TPLACE[dz]).start()

    def txt_wait(r):
        for move in TXT_OUT[r]:
            txt_copy(move).wait_recv()

    def sib_wait(r):
        for dz in FRESH[r]:
            sib_copy(TPLACE[dz]).wait_recv()

    def ids_of(slots, base):
        pair = slots[pl.ds(base + D, 16), :].astype(jnp.float32)
        return pair[0:1, :] * 64.0 + pair[1:2, :]

    def take_img(first, count):
        def body(s, carry):
            base = pl.multiple_of(s * BLOCK, 16)
            rows = pl.ds(pl.multiple_of(s * 128, 128), 128)
            for c in range(TILES):
                img[rows, c * 128 : (c + 1) * 128] = irx[pl.ds(base + c * 128, 128), :]
            idi[rows, :] = jnp.broadcast_to(ids_of(irx, base), (128, 128)).T
            return carry
        lax.fori_loop(first, first + count, body, 0)

    def take_txt(places, lane):
        for k in places:
            slot = 2 * k + lane
            base = (8 * lane + k) * BLOCK
            for c in range(TILES):
                txt[slot * 128 : (slot + 1) * 128, c * 128 : (c + 1) * 128] = trx[
                    pl.ds(base + c * 128, 128), :
                ]
            idt[:, slot * 128 : (slot + 1) * 128] = ids_of(trx, base)

    scale = sharp_ref[0] * (1.0 / math.log(2.0))
    shift = offset_ref[0] * (1.0 / math.log(2.0))

    def pairs(i0, ni, j0, nj):
        rows, cols = pl.ds(i0, ni), pl.ds(j0, nj)
        dots = lax.dot_general(
            img[rows, :], txt[cols, :], (((1,), (1,)), ((), ())),
            preferred_element_type=jnp.float32,
        )
        logits = dots * scale + shift
        match = jnp.concatenate([idi[rows, :]] * (nj // 128), axis=1) == idt[:, cols]
        power = jnp.exp2(jnp.where(match, -logits, logits))
        whole = 1.0 + power
        part = power * pl.reciprocal(whole, approx=True)
        weights = jnp.where(match, -part, part).astype(jnp.bfloat16)
        terms = jnp.log2(whole).reshape(ni // 8, 8, nj).sum(axis=0)
        total[...] += sum(terms[:, c * 128 : (c + 1) * 128] for c in range(nj // 128))
        gi[rows, :] += jnp.dot(weights, txt[cols, :], preferred_element_type=jnp.float32)
        gt[cols, :] += lax.dot_general(
            weights, img[rows, :], (((0,), (0,)), ((), ())),
            preferred_element_type=jnp.float32,
        )

    def pack(acc, block, out, base, lo, hi):
        for tile, first, end in spans(lo, hi):
            out[pl.ds(base + tile * 128 + first, end - first), :] = acc[
                pl.ds(block * 128 + first, end - first), tile * 128 : (tile + 1) * 128
            ].astype(jnp.bfloat16)

    def fold(acc, block, land, base, lo, hi):
        for tile, first, end in spans(lo, hi):
            rows = pl.ds(block * 128 + first, end - first)
            acc[rows, tile * 128 : (tile + 1) * 128] += land[
                pl.ds(base + tile * 128 + first - lo, end - first), :
            ].astype(jnp.float32)

    def img_back(move):
        k, slot, _, lo, hi, direction, land = move
        return remote(
            isend.at[pl.ds(slot * D + lo, hi - lo)], iland.at[pl.ds(land, hi - lo)],
            is_s.at[k], is_r.at[k], near[direction],
        )

    def txt_back(move):
        k, slot, _, lo, hi, direction, land = move
        return remote(
            tsend.at[pl.ds(slot * D + lo, hi - lo)], tland.at[pl.ds(land, hi - lo)],
            ts_s.at[k], ts_r.at[k], near[direction],
        )

    def sib_back(k):
        return remote(
            ssend.at[pl.ds(k * D, D)], sland.at[pl.ds(k * D, D)], ss_s.at[k], ss_r.at[k], sib
        )

    def img_give(r):
        for move in IMG_BACK[r]:
            _, slot, _, lo, hi, _, _ = move
            pack(gi, slot, isend, slot * D, lo, hi)
            img_back(move).start()

    def img_add(r):
        for move in IMG_BACK[r]:
            _, _, slot, lo, hi, _, land = move
            img_back(move).wait_recv()
            fold(gi, slot, iland, land, lo, hi)

    def sib_give(r):
        for dz in FRESH[r]:
            k = TPLACE[dz]
            pack(gt, 2 * k + 1, ssend, k * D, 0, D)
            sib_back(k).start()

    def sib_add(r):
        for dz in FRESH[r]:
            k = TPLACE[dz]
            sib_back(k).wait_recv()
            fold(gt, 2 * k, sland, k * D, 0, D)

    def txt_give(r):
        for move in TXT_BACK[r]:
            _, slot, _, lo, hi, _, _ = move
            pack(gt, 2 * slot, tsend, slot * D, lo, hi)
            txt_back(move).start()

    def txt_add(r):
        for move in TXT_BACK[r]:
            _, _, slot, lo, hi, _, land = move
            txt_back(move).wait_recv()
            fold(gt, 2 * slot, tland, land, lo, hi)

    def loss_copies(step):
        buf, me, devices, first = (
            (lc, core, [sib], 0), (lx, x, xs[1:], 1), (ly, y, ys[1:], 4), (lz, z, zs[1:], 7)
        )[step]
        copies = [
            remote(buf.at[me], buf.at[me], l_s.at[first + k], l_r.at[first + k], device)
            for k, device in enumerate(devices)
        ]
        return buf, me, copies

    def loss_give(step, value):
        buf, me, copies = loss_copies(step)
        buf[me] = value
        for copy in copies:
            copy.start()

    def loss_take(step):
        buf, _, copies = loss_copies(step)
        for copy in copies:
            copy.wait_recv()
        return sum(buf[k] for k in range(buf.shape[0]))

    img_start(0)
    txt_start(0)
    gi[...] = jnp.zeros_like(gi)
    gt[...] = jnp.zeros_like(gt)
    total[...] = jnp.zeros_like(total)
    take_img(0, 1)
    take_txt([0], 0)
    sib_wait(0)
    take_txt([0], 1)

    def arrive(r):
        img_wait(r)
        if r < 3:
            img_start(r + 1)
        txt_wait(r)
        txt_start(r + 1)
        first, count = ((1, 4), (5, 6), (11, 4), (15, 1))[r]
        take_img(first, count)
        places = [TPLACE[dz] for dz in FRESH[r + 1]]
        take_txt(places, 0)
        sib_wait(r + 1)
        take_txt(places, 1)

    for r in range(4):
        arrive(r)
    for i0 in (0, 1024):
        for j0 in (0, 1024):
            pairs(i0, 1024, j0, 1024)

    loss_give(0, total[...])
    img_give(3)
    sib_give(4)
    sib_give(3)
    sib_add(4)
    txt_give(3)
    sib_add(3)
    sib_give(2)
    sib_give(1)
    img_add(3)
    img_give(2)
    loss_give(1, loss_take(0))
    txt_add(3)
    txt_give(2)
    sib_give(0)
    sib_add(2)
    sib_add(1)
    sib_add(0)
    loss_give(2, loss_take(1))
    txt_add(2)
    txt_give(1)
    img_add(2)
    img_give(1)
    loss_give(3, loss_take(2))
    txt_add(1)
    txt_give(0)
    img_add(1)
    img_give(0)
    loss_ref[0] = jnp.sum(loss_take(3)) * (math.log(2.0) / BATCH)
    txt_add(0)

    def finish(ref, acc, out):
        unit, norm = unit32(ref)
        grad = acc[pl.ds(0, 128), :] * sharp_ref[0]
        along = jnp.sum(unit * grad, axis=-1, keepdims=True)
        out[...] = ((grad - unit * along) / norm).astype(jnp.bfloat16)

    finish(footage_ref, gt, gtxt_ref)
    img_add(0)
    finish(echo_ref, gi, gimg_ref)

    for r in range(4):
        for move in IMG_OUT[r]:
            img_copy(move).wait_send()
        for move in TXT_OUT[r]:
            txt_copy(move).wait_send()
        for move in IMG_BACK[r]:
            img_back(move).wait_send()
        for move in TXT_BACK[r]:
            txt_back(move).wait_send()
        for copy in loss_copies(r)[2]:
            copy.wait_send()
    for k in range(8):
        sib_copy(k).wait_send()
        sib_back(k).wait_send()


def per_device(echo_vectors, footage_vectors, match_numbers, sharpness_factor, score_offset):
    bf16, f32 = jnp.bfloat16, jnp.float32
    vmem = pl.BlockSpec(memory_space=pltpu.VMEM)
    smem = pl.BlockSpec(memory_space=pltpu.SMEM)
    dma = pltpu.SemaphoreType.DMA
    grad_image, grad_text, loss = pl.pallas_call(
        kernel,
        name="contrastive_step",
        out_shape=[
            jax.ShapeDtypeStruct((ROWS, D), bf16),
            jax.ShapeDtypeStruct((ROWS, D), bf16),
            jax.ShapeDtypeStruct((1,), f32),
        ],
        in_specs=[vmem, vmem, vmem, smem, smem],
        out_specs=[vmem, vmem, smem],
        scratch_shapes=[
            pltpu.VMEM((SLOTS * BLOCK, 128), bf16),
            pltpu.VMEM((SLOTS * BLOCK, 128), bf16),
            pltpu.VMEM((N, D), bf16),
            pltpu.VMEM((N, D), bf16),
            pltpu.VMEM((N, 128), f32),
            pltpu.VMEM((1, N), f32),
            pltpu.VMEM((N, D), f32),
            pltpu.VMEM((N, D), f32),
            pltpu.VMEM((SLOTS * D, 128), bf16),
            pltpu.VMEM((IMG_LAND, 128), bf16),
            pltpu.VMEM((8 * D, 128), bf16),
            pltpu.VMEM((TXT_LAND, 128), bf16),
            pltpu.VMEM((8 * D, 128), bf16),
            pltpu.VMEM((8 * D, 128), bf16),
            pltpu.VMEM((8, 128), f32),
            pltpu.VMEM((2, 8, 128), f32),
            pltpu.VMEM((4, 8, 128), f32),
            pltpu.VMEM((4, 8, 128), f32),
            pltpu.VMEM((8, 8, 128), f32),
            dma((IMG_N,)), dma((IMG_N,)),
            dma((TXT_N,)), dma((TXT_N,)),
            dma((8,)), dma((8,)),
            dma((IMG_N,)), dma((IMG_N,)),
            dma((TXT_N,)), dma((TXT_N,)),
            dma((8,)), dma((8,)),
            dma((14,)), dma((14,)),
        ],
        compiler_params=pltpu.CompilerParams(
            collective_id=0, has_side_effects=True, vmem_limit_bytes=60 << 20
        ),
    )(echo_vectors, footage_vectors, match_numbers.reshape(1, ROWS), sharpness_factor, score_offset)
    return grad_image, grad_text, loss


def solution(mesh):
    return jax.shard_map(
        per_device,
        mesh=mesh,
        in_specs=(
            P(("blk", "inner"), None),
            P(("blk", "inner"), None),
            P(("blk", "inner")),
            P(),
            P(),
        ),
        out_specs=(P(("blk", "inner"), None), P(("blk", "inner"), None), P()),
        check_vma=False,
    )
```

```python
import functools
import math

import jax
import jax.numpy as jnp
from jax import lax
from jax.experimental import pallas as pl
from jax.experimental.pallas import tpu as pltpu
from jax.sharding import PartitionSpec as P

ROWS, D = 128, 768
TILES = D // 128
BLOCK = D + 16
SLOTS = 16
N = SLOTS * ROWS
BATCH = 32768
MESH = pl.DeviceIdType.MESH

A, B = (0, 384), (384, BLOCK)
A0, A1, B0, B1 = (0, 192), (192, 384), (384, 576), (576, BLOCK)

PLACES = [
    (0, 0), (1, 0), (3, 0), (0, 1), (0, 3),
    (2, 0), (0, 2), (1, 1), (1, 3), (3, 1), (3, 3),
    (2, 1), (2, 3), (1, 2), (3, 2), (2, 2),
]
ISLOT = {place: slot for slot, place in enumerate(PLACES)}
STEP = {"+x": (1, 0), "-x": (3, 0), "+y": (0, 1), "-y": (0, 3)}
BACK = {"+x": "-x", "-x": "+x", "+y": "-y", "-y": "+y", "+z": "-z", "-z": "+z"}
IMG = [
    [
        ((0, 0), A, "+x"), ((0, 0), A, "-x"), ((0, 0), B, "+y"), ((0, 0), B, "-y"),
        ((0, 0), B, "+x"), ((0, 0), B, "-x"), ((0, 0), A, "+y"), ((0, 0), A, "-y"),
    ],
    [
        ((3, 0), A, "+x"), ((0, 1), B, "-x"), ((1, 0), A, "+y"), ((0, 1), B, "-y"),
        ((0, 1), B, "+x"), ((1, 0), A, "-y"),
    ],
    [
        ((1, 0), B, "-x"), ((0, 3), A, "+y"), ((0, 3), B, "+x"), ((3, 0), A, "-y"),
        ((0, 3), B, "-x"), ((3, 0), A, "+y"),
    ],
    [
        ((0, 2), B, "+x"), ((0, 2), B, "-x"), ((2, 0), A, "+y"), ((2, 0), A, "-y"),
        ((1, 1), B1, "-x"), ((1, 3), A0, "+y"),
    ],
    [((3, 1), B0, "+x"), ((1, 1), A1, "-y")],
    [((3, 3), B0, "+x"), ((1, 3), B1, "-x"), ((3, 3), A0, "+y"), ((3, 1), A1, "-y")],
    [((3, 2), B0, "+x"), ((1, 2), B1, "-x"), ((2, 3), A0, "+y"), ((2, 1), A1, "-y")],
]
DZ = [0, 1, 7, 2, 6, 3, 5, 4]
TPLACE = {dz: k for k, dz in enumerate(DZ)}
TORDER = [
    (0, 0), (0, 1), (1, 0), (7, 0), (1, 1), (7, 1), (2, 0), (6, 0), (2, 1), (6, 1),
    (3, 0), (5, 0), (3, 1), (5, 1), (4, 0), (4, 1),
]
TSLOT = {place: slot for slot, place in enumerate(TORDER)}
TXT = [
    [(0, A, "+z"), (0, B, "-z"), (0, B, "+z"), (0, A, "-z")],
    [(7, A, "+z"), (1, B, "-z")],
    [(7, B, "+z"), (1, A, "-z")],
    [(6, A, "+z"), (2, B, "-z")],
    [(6, B, "+z"), (2, A, "-z")],
    [(5, A, "+z"), (3, B, "-z")],
]


def img_to(place, direction):
    sx, sy = STEP[direction]
    return ((place[0] - sx) % 4, (place[1] - sy) % 4)


def txt_to(dz, direction):
    return (dz - 1) % 8 if direction == "+z" else (dz + 1) % 8


def numbered(rounds, to, slot_of):
    gather, scatter, count, land = [], [], 0, 0
    for moves in rounds:
        out, back = [], []
        for place, (lo, hi), direction in moves:
            there = to(place, direction)
            out.append((count, slot_of[place], slot_of[there], lo, hi, direction))
            top = min(hi, D)
            back.append((count, slot_of[there], slot_of[place], lo, top, BACK[direction], land))
            land += top - lo
            count += 1
        gather.append(out)
        scatter.append(back)
    return gather, scatter, count, land


IMG_OUT, IMG_BACK, IMG_N, IMG_LAND = numbered(IMG, img_to, ISLOT)
TXT_OUT, TXT_BACK, TXT_N, TXT_LAND = numbered(TXT, txt_to, TPLACE)


def spans(lo, hi):
    edges = [e for e in range(0, D + 1, 64) if lo <= e <= hi and (e % 128 == 0 or e % 192 == 0)]
    return list(zip(edges[:-1], edges[1:]))


def incoming(rounds):
    found = {}
    for moves in rounds:
        for _, _, slot, lo, hi, _, land in moves:
            found.setdefault(slot, []).append((lo, hi, land))
    return found


IMG_IN, TXT_IN = incoming(IMG_BACK), incoming(TXT_BACK)


def kernel(
    echo_ref, footage_ref, ids_ref, sharp_ref, offset_ref,
    gimg_ref, gtxt_ref, loss_ref,
    irx, trx, img, txt, idi, idt, gi, gt,
    isend, iland, tsend, tland, ssend, sland,
    total, lc, lx, ly, lz,
    ig_s, ig_r, tg_s, tg_r, sg_s, sg_r,
    is_s, is_r, ts_s, ts_r, ss_s, ss_r, l_s, l_r,
):
    blk, inner = lax.axis_index("blk"), lax.axis_index("inner")
    core = lax.rem(blk, 2)
    z = lax.div(blk, 4)
    x = lax.rem(inner, 2) * 2 + lax.rem(lax.div(blk, 2), 2)
    y = lax.div(inner, 2)

    def at(z, x, y, core):
        return {
            "blk": z * 4 + lax.rem(x, 2) * 2 + core,
            "inner": y * 2 + lax.div(x, 2),
        }

    xs = [at(z, lax.rem(x + k, 4), y, core) for k in range(4)]
    ys = [at(z, x, lax.rem(y + k, 4), core) for k in range(4)]
    zs = [at(lax.rem(z + k, 8), x, y, core) for k in range(8)]
    sib = at(z, x, y, 1 - core)
    near = {"+x": xs[1], "-x": xs[3], "+y": ys[1], "-y": ys[3], "+z": zs[1], "-z": zs[7]}

    barrier = pltpu.get_barrier_semaphore()
    partners = xs[1:] + ys[1:] + zs[1:] + [sib]
    for device in partners:
        pl.semaphore_signal(barrier, inc=1, device_id=device, device_id_type=MESH)

    def unit32(ref):
        values = ref[...].astype(jnp.float32)
        norm = jnp.sqrt(jnp.sum(values * values, axis=-1, keepdims=True) + 1e-06)
        return values / norm, norm

    ids = ids_ref[...]
    row = lax.broadcasted_iota(jnp.int32, (16, 128), 0)
    high = jnp.broadcast_to((ids >> 6).astype(jnp.float32), (16, 128))
    low = jnp.broadcast_to((ids & 63).astype(jnp.float32), (16, 128))
    id_rows = jnp.where(row == 0, high, jnp.where(row == 1, low, 0.0)).astype(jnp.bfloat16)
    for ref, slots in ((echo_ref, irx), (footage_ref, trx)):
        unit = unit32(ref)[0].astype(jnp.bfloat16)
        for c in range(TILES):
            slots[pl.ds(c * 128, 128), :] = unit[:, c * 128 : (c + 1) * 128]
        slots[pl.ds(D, 16), :] = id_rows

    pl.semaphore_wait(barrier, len(partners))

    def remote(src, dst, send, recv, device):
        return pltpu.make_async_remote_copy(
            src_ref=src, dst_ref=dst, send_sem=send, recv_sem=recv,
            device_id=device, device_id_type=MESH,
        )

    def img_copy(move):
        k, slot, there, lo, hi, direction = move
        return remote(
            irx.at[pl.ds(slot * BLOCK + lo, hi - lo)], irx.at[pl.ds(there * BLOCK + lo, hi - lo)],
            ig_s.at[k], ig_r.at[k], near[direction],
        )

    def txt_copy(move):
        k, slot, there, lo, hi, direction = move
        return remote(
            trx.at[pl.ds(slot * BLOCK + lo, hi - lo)], trx.at[pl.ds(there * BLOCK + lo, hi - lo)],
            tg_s.at[k], tg_r.at[k], near[direction],
        )

    def sib_copy(k):
        return remote(
            trx.at[pl.ds(k * BLOCK, BLOCK)], trx.at[pl.ds((8 + k) * BLOCK, BLOCK)],
            sg_s.at[k], sg_r.at[k], sib,
        )

    def start(copy, moves):
        for move in moves:
            copy(move).start()

    def arrived(copy, moves):
        for move in moves:
            copy(move).wait_recv()

    def sib_start(*places):
        for dz in places:
            sib_copy(TPLACE[dz]).start()

    def sib_wait(*places):
        for dz in places:
            sib_copy(TPLACE[dz]).wait_recv()

    def ids_of(slots, base):
        pair = slots[pl.ds(base + D, 16), :].astype(jnp.float32)
        return pair[0:1, :] * 64.0 + pair[1:2, :]

    def take_img(first, count):
        def body(s, carry):
            base = pl.multiple_of(s * BLOCK, 16)
            rows = pl.ds(pl.multiple_of(s * 128, 128), 128)
            for c in range(TILES):
                img[rows, c * 128 : (c + 1) * 128] = irx[pl.ds(base + c * 128, 128), :]
            idi[rows, :] = jnp.broadcast_to(ids_of(irx, base), (128, 128)).T
            return carry
        lax.fori_loop(first, first + count, body, 0)

    def take_txt(lane, *places):
        for dz in places:
            k, slot = TPLACE[dz], TSLOT[dz, lane]
            base = (8 * lane + k) * BLOCK
            for c in range(TILES):
                txt[slot * 128 : (slot + 1) * 128, c * 128 : (c + 1) * 128] = trx[
                    pl.ds(base + c * 128, 128), :
                ]
            idt[:, slot * 128 : (slot + 1) * 128] = ids_of(trx, base)

    scale = sharp_ref[0] * (1.0 / math.log(2.0))
    shift = offset_ref[0] * (1.0 / math.log(2.0))

    def pairs(i0, ni, j0, nj):
        rows, cols = pl.ds(i0, ni), pl.ds(j0, nj)
        dots = lax.dot_general(
            img[rows, :], txt[cols, :], (((1,), (1,)), ((), ())),
            preferred_element_type=jnp.float32,
        )
        logits = dots * scale + shift
        match = jnp.concatenate([idi[rows, :]] * (nj // 128), axis=1) == idt[:, cols]
        power = jnp.exp2(jnp.where(match, -logits, logits))
        whole = 1.0 + power
        part = power * pl.reciprocal(whole, approx=True)
        weights = jnp.where(match, -part, part).astype(jnp.bfloat16)
        terms = jnp.log2(whole).reshape(ni // 8, 8, nj).sum(axis=0)
        total[...] += sum(terms[:, c * 128 : (c + 1) * 128] for c in range(nj // 128))
        gi[rows, :] += jnp.dot(weights, txt[cols, :], preferred_element_type=jnp.float32)
        gt[cols, :] += lax.dot_general(
            weights, img[rows, :], (((0,), (0,)), ((), ())),
            preferred_element_type=jnp.float32,
        )

    def summed(acc, block, lo, hi, lands):
        tile, first = lo // 128, lo % 128
        value = acc[
            pl.ds(block * 128 + first, hi - lo), tile * 128 : (tile + 1) * 128
        ]
        for land, base, top, end in lands:
            if top <= lo and hi <= end:
                value = value + land[pl.ds(base + lo - top, hi - lo), :].astype(jnp.float32)
        return value

    def img_lands(slot):
        return [(iland, base, lo, hi) for lo, hi, base in IMG_IN.get(slot, [])]

    def txt_lands(k):
        return [(sland, k * D, 0, D)] + [
            (tland, base, lo, hi) for lo, hi, base in TXT_IN.get(k, [])
        ]

    def pack(acc, block, out, base, lo, hi, lands):
        for first, end in spans(lo, hi):
            out[pl.ds(base + first, end - first), :] = summed(
                acc, block, first, end, lands
            ).astype(jnp.bfloat16)

    def img_back(move):
        k, slot, _, lo, hi, direction, land = move
        return remote(
            isend.at[pl.ds(slot * D + lo, hi - lo)], iland.at[pl.ds(land, hi - lo)],
            is_s.at[k], is_r.at[k], near[direction],
        )

    def txt_back(move):
        k, slot, _, lo, hi, direction, land = move
        return remote(
            tsend.at[pl.ds(slot * D + lo, hi - lo)], tland.at[pl.ds(land, hi - lo)],
            ts_s.at[k], ts_r.at[k], near[direction],
        )

    def sib_back(k):
        return remote(
            ssend.at[pl.ds(k * D, D)], sland.at[pl.ds(k * D, D)], ss_s.at[k], ss_r.at[k], sib
        )

    def img_give(moves):
        for move in moves:
            _, slot, _, lo, hi, _, _ = move
            pack(gi, slot, isend, slot * D, lo, hi, img_lands(slot))
            img_back(move).start()

    def sib_give(*places):
        for dz in places:
            k = TPLACE[dz]
            pack(gt, TSLOT[dz, 1], ssend, k * D, 0, D, [])
            sib_back(k).start()

    def sib_got(*places):
        for dz in places:
            sib_back(TPLACE[dz]).wait_recv()

    def txt_give(moves):
        for move in moves:
            _, k, _, lo, hi, _, _ = move
            pack(gt, TSLOT[DZ[k], 0], tsend, k * D, lo, hi, txt_lands(k))
            txt_back(move).start()

    def loss_copies(step):
        buf, me, devices, first = (
            (lc, core, [sib], 0), (lx, x, xs[1:], 1), (ly, y, ys[1:], 4), (lz, z, zs[1:], 7)
        )[step]
        copies = [
            remote(buf.at[me], buf.at[me], l_s.at[first + k], l_r.at[first + k], device)
            for k, device in enumerate(devices)
        ]
        return buf, me, copies

    def loss_give(step, value):
        buf, me, copies = loss_copies(step)
        buf[me] = value
        for copy in copies:
            copy.start()

    def loss_take(step):
        buf, _, copies = loss_copies(step)
        for copy in copies:
            copy.wait_recv()
        return sum(buf[k] for k in range(buf.shape[0]))

    I, T, IB, TB = IMG_OUT, TXT_OUT, IMG_BACK, TXT_BACK
    start(img_copy, I[0][:4])
    start(txt_copy, T[0][:2])
    start(img_copy, I[0][4:])
    start(txt_copy, T[0][2:])
    sib_start(0)
    gi[...] = jnp.zeros_like(gi)
    gt[...] = jnp.zeros_like(gt)
    total[...] = jnp.zeros_like(total)
    take_img(0, 1)
    take_txt(0, 0)

    arrived(img_copy, I[0][:4])
    start(img_copy, I[1])
    arrived(txt_copy, T[0][:2])
    start(txt_copy, T[1])
    sib_wait(0)
    take_txt(1, 0)

    arrived(img_copy, I[0][4:])
    start(img_copy, I[2])
    arrived(txt_copy, T[0][2:])
    start(txt_copy, T[2])
    sib_start(1, 7)
    take_img(1, 4)
    take_txt(0, 1, 7)
    pairs(0, 640, 0, 512)

    arrived(img_copy, I[1][:4])
    start(img_copy, I[3])
    arrived(txt_copy, T[1])
    start(txt_copy, T[3])
    sib_wait(1, 7)
    take_txt(1, 1, 7)
    pairs(0, 640, 512, 256)

    arrived(img_copy, I[1][4:])
    start(img_copy, I[4])
    arrived(txt_copy, T[2])
    start(txt_copy, T[4])
    sib_start(2, 6)
    take_txt(0, 2, 6)
    pairs(0, 640, 768, 256)

    arrived(img_copy, I[2])
    start(img_copy, I[5])
    arrived(txt_copy, T[3])
    start(txt_copy, T[5])
    take_img(5, 6)
    pairs(640, 768, 0, 512)

    arrived(img_copy, I[3][:4])
    start(img_copy, I[6])
    arrived(txt_copy, T[4])
    sib_start(3, 5)
    sib_wait(2, 6)
    take_txt(1, 2, 6)
    pairs(640, 768, 512, 512)

    arrived(txt_copy, T[5])
    sib_start(4)
    pairs(0, 1408, 1024, 256)

    for moves in (I[3][4:], I[4], I[5], I[6]):
        arrived(img_copy, moves)
    take_img(11, 5)
    pairs(1408, 640, 0, 1280)
    take_txt(0, 3, 5, 4)
    sib_wait(3, 5, 4)
    take_txt(1, 3, 5, 4)
    sib_give(2, 6, 1, 7, 0)
    pairs(1408, 640, 1280, 768)
    img_give(IB[6])
    for moves in (IB[5], IB[4], IB[3][4:]):
        img_give(moves)
    pairs(0, 1408, 1792, 256)
    sib_give(4)
    sib_got(2, 6, 1, 7, 0)
    pairs(640, 768, 1280, 512)
    arrived(img_back, IB[6])
    img_give(IB[3][:4])
    for moves in (IB[5], IB[4], IB[3][4:]):
        arrived(img_back, moves)
    first = [IB[1][1], IB[2][2], IB[2][3], IB[1][2], IB[2][4], IB[1][4], IB[1][5], IB[2][5]]
    third = [IB[2][0], IB[2][1]]
    late = [IB[1][0], IB[1][3]]
    img_give(first)
    img_give(third)
    sib_got(4)
    txt_give(TB[5])
    pairs(0, 640, 1280, 512)

    sib_give(3, 5)
    loss_give(0, total[...])
    home = {(slot, lo): move for move in IB[0] for _, slot, _, lo, _, _, _ in [move]}
    arrived(img_back, IB[3][:4])
    img_give(late)
    img_give([home[2, 384], home[3, 0]])
    sib_got(3, 5)
    txt_give(TB[4])
    arrived(txt_back, TB[5])
    txt_give(TB[3])
    loss_give(1, loss_take(0))
    arrived(img_back, first)
    img_give([home[1, 0], home[4, 384]])
    arrived(txt_back, TB[4])
    txt_give(TB[2])
    loss_give(2, loss_take(1))
    arrived(img_back, third)
    img_give([home[1, 384], home[4, 0]])
    arrived(txt_back, TB[3])
    txt_give(TB[1])
    arrived(img_back, late)
    img_give([home[2, 0], home[3, 384]])
    loss_give(3, loss_take(2))
    arrived(txt_back, TB[2])
    txt_give(TB[0][2:])
    arrived(txt_back, TB[1])
    txt_give(TB[0][:2])
    loss_ref[0] = jnp.sum(loss_take(3)) * (math.log(2.0) / BATCH)

    def finish(ref, acc, lands, out):
        unit, norm = unit32(ref)
        tiles = [summed(acc, 0, c * 128, (c + 1) * 128, lands) for c in range(TILES)]
        grad = jnp.concatenate(tiles, axis=1) * sharp_ref[0]
        along = jnp.sum(unit * grad, axis=-1, keepdims=True)
        out[...] = ((grad - unit * along) / norm).astype(jnp.bfloat16)

    arrived(img_back, IB[0])
    finish(echo_ref, gi, img_lands(0), gimg_ref)
    arrived(txt_back, TB[0])
    finish(footage_ref, gt, txt_lands(0), gtxt_ref)

    for moves in I:
        for move in moves:
            img_copy(move).wait_send()
    for moves in T:
        for move in moves:
            txt_copy(move).wait_send()
    for moves in IB:
        for move in moves:
            img_back(move).wait_send()
    for moves in TB:
        for move in moves:
            txt_back(move).wait_send()
    for r in range(4):
        for copy in loss_copies(r)[2]:
            copy.wait_send()
    for k in range(8):
        sib_copy(k).wait_send()
        sib_back(k).wait_send()


def per_device(echo_vectors, footage_vectors, match_numbers, sharpness_factor, score_offset):
    bf16, f32 = jnp.bfloat16, jnp.float32
    vmem = pl.BlockSpec(memory_space=pltpu.VMEM)
    smem = pl.BlockSpec(memory_space=pltpu.SMEM)
    dma = pltpu.SemaphoreType.DMA
    grad_image, grad_text, loss = pl.pallas_call(
        kernel,
        name="contrastive_step",
        out_shape=[
            jax.ShapeDtypeStruct((ROWS, D), bf16),
            jax.ShapeDtypeStruct((ROWS, D), bf16),
            jax.ShapeDtypeStruct((1,), f32),
        ],
        in_specs=[vmem, vmem, vmem, smem, smem],
        out_specs=[vmem, vmem, smem],
        scratch_shapes=[
            pltpu.VMEM((SLOTS * BLOCK, 128), bf16),
            pltpu.VMEM((SLOTS * BLOCK, 128), bf16),
            pltpu.VMEM((N, D), bf16),
            pltpu.VMEM((N, D), bf16),
            pltpu.VMEM((N, 128), f32),
            pltpu.VMEM((1, N), f32),
            pltpu.VMEM((N, D), f32),
            pltpu.VMEM((N, D), f32),
            pltpu.VMEM((SLOTS * D, 128), bf16),
            pltpu.VMEM((IMG_LAND, 128), bf16),
            pltpu.VMEM((8 * D, 128), bf16),
            pltpu.VMEM((TXT_LAND, 128), bf16),
            pltpu.VMEM((8 * D, 128), bf16),
            pltpu.VMEM((8 * D, 128), bf16),
            pltpu.VMEM((8, 128), f32),
            pltpu.VMEM((2, 8, 128), f32),
            pltpu.VMEM((4, 8, 128), f32),
            pltpu.VMEM((4, 8, 128), f32),
            pltpu.VMEM((8, 8, 128), f32),
            dma((IMG_N,)), dma((IMG_N,)),
            dma((TXT_N,)), dma((TXT_N,)),
            dma((8,)), dma((8,)),
            dma((IMG_N,)), dma((IMG_N,)),
            dma((TXT_N,)), dma((TXT_N,)),
            dma((8,)), dma((8,)),
            dma((14,)), dma((14,)),
        ],
        compiler_params=pltpu.CompilerParams(
            collective_id=0, has_side_effects=True, vmem_limit_bytes=60 << 20
        ),
    )(echo_vectors, footage_vectors, match_numbers.reshape(1, ROWS), sharpness_factor, score_offset)
    return grad_image, grad_text, loss


def solution(mesh):
    return jax.shard_map(
        per_device,
        mesh=mesh,
        in_specs=(
            P(("blk", "inner"), None),
            P(("blk", "inner"), None),
            P(("blk", "inner")),
            P(),
            P(),
        ),
        out_specs=(P(("blk", "inner"), None), P(("blk", "inner"), None), P()),
        check_vma=False,
    )
```

```python
import functools
import math

import jax
import jax.numpy as jnp
from jax import lax
from jax.experimental import pallas as pl
from jax.experimental.pallas import tpu as pltpu
from jax.sharding import PartitionSpec as P

ROWS, D = 128, 768
TILES = D // 128
BLOCK = D + 16
SLOTS = 16
N = SLOTS * ROWS
BATCH = 32768
MESH = pl.DeviceIdType.MESH

A, B = (0, 384), (384, BLOCK)
A0, A1, B0, B1 = (0, 192), (192, 384), (384, 576), (576, BLOCK)

PLACES = [
    (0, 0), (1, 0), (3, 0), (0, 1), (0, 3),
    (2, 0), (0, 2), (1, 1), (1, 3), (3, 1), (3, 3),
    (2, 1), (2, 3), (1, 2), (3, 2), (2, 2),
]
ISLOT = {place: slot for slot, place in enumerate(PLACES)}
STEP = {"+x": (1, 0), "-x": (3, 0), "+y": (0, 1), "-y": (0, 3)}
BACK = {"+x": "-x", "-x": "+x", "+y": "-y", "-y": "+y", "+z": "-z", "-z": "+z"}
IMG = [
    [
        ((0, 0), A, "+x"), ((0, 0), A, "-x"), ((0, 0), B, "+y"), ((0, 0), B, "-y"),
        ((0, 0), B, "+x"), ((0, 0), B, "-x"), ((0, 0), A, "+y"), ((0, 0), A, "-y"),
    ],
    [
        ((3, 0), A, "+x"), ((0, 1), B, "-x"), ((1, 0), A, "+y"), ((0, 1), B, "-y"),
        ((0, 1), B, "+x"), ((1, 0), A, "-y"),
    ],
    [
        ((1, 0), B, "-x"), ((0, 3), A, "+y"), ((0, 3), B, "+x"), ((3, 0), A, "-y"),
        ((0, 3), B, "-x"), ((3, 0), A, "+y"),
    ],
    [
        ((0, 2), B, "+x"), ((0, 2), B, "-x"), ((2, 0), A, "+y"), ((2, 0), A, "-y"),
        ((1, 1), B1, "-x"), ((1, 3), A0, "+y"),
    ],
    [((3, 1), B0, "+x"), ((1, 1), A1, "-y")],
    [((3, 3), B0, "+x"), ((1, 3), B1, "-x"), ((3, 3), A0, "+y"), ((3, 1), A1, "-y")],
    [((3, 2), B0, "+x"), ((1, 2), B1, "-x"), ((2, 3), A0, "+y"), ((2, 1), A1, "-y")],
]
DZ = [0, 1, 7, 2, 6, 3, 5, 4]
TPLACE = {dz: k for k, dz in enumerate(DZ)}
TORDER = [
    (0, 0), (0, 1), (1, 0), (7, 0), (1, 1), (7, 1), (2, 0), (6, 0), (2, 1), (6, 1),
    (3, 0), (5, 0), (3, 1), (5, 1), (4, 0), (4, 1),
]
TSLOT = {place: slot for slot, place in enumerate(TORDER)}
TXT = [
    [(0, A, "+z"), (0, B, "-z"), (0, B, "+z"), (0, A, "-z")],
    [(7, A, "+z"), (1, B, "-z")],
    [(7, B, "+z"), (1, A, "-z")],
    [(6, A, "+z"), (2, B, "-z")],
    [(6, B, "+z"), (2, A, "-z")],
    [(5, A, "+z"), (3, B, "-z")],
]


def img_to(place, direction):
    sx, sy = STEP[direction]
    return ((place[0] - sx) % 4, (place[1] - sy) % 4)


def txt_to(dz, direction):
    return (dz - 1) % 8 if direction == "+z" else (dz + 1) % 8


def numbered(rounds, to, slot_of):
    gather, scatter, count, land = [], [], 0, 0
    for moves in rounds:
        out, back = [], []
        for place, (lo, hi), direction in moves:
            there = to(place, direction)
            out.append((count, slot_of[place], slot_of[there], lo, hi, direction))
            top = min(hi, D)
            back.append((count, slot_of[there], slot_of[place], lo, top, BACK[direction], land))
            land += top - lo
            count += 1
        gather.append(out)
        scatter.append(back)
    return gather, scatter, count, land


IMG_OUT, IMG_BACK, IMG_N, IMG_LAND = numbered(IMG, img_to, ISLOT)
TXT_OUT, TXT_BACK, TXT_N, TXT_LAND = numbered(TXT, txt_to, TPLACE)


def spans(lo, hi):
    edges = [e for e in range(0, D + 1, 64) if lo <= e <= hi and (e % 128 == 0 or e % 192 == 0)]
    return list(zip(edges[:-1], edges[1:]))


def incoming(rounds):
    found = {}
    for moves in rounds:
        for _, _, slot, lo, hi, _, land in moves:
            found.setdefault(slot, []).append((lo, hi, land))
    return found


IMG_IN, TXT_IN = incoming(IMG_BACK), incoming(TXT_BACK)


def kernel(
    echo_ref, footage_ref, ids_ref, sharp_ref, offset_ref,
    gimg_ref, gtxt_ref, loss_ref,
    irx, trx, img, txt, idi, idt, gi, gt,
    isend, iland, tsend, tland, ssend, sland,
    total, lc, lx, ly, lz,
    ig_s, ig_r, tg_s, tg_r, sg_s, sg_r,
    is_s, is_r, ts_s, ts_r, ss_s, ss_r, l_s, l_r,
):
    blk, inner = lax.axis_index("blk"), lax.axis_index("inner")
    core = lax.rem(blk, 2)
    z = lax.div(blk, 4)
    x = lax.rem(inner, 2) * 2 + lax.rem(lax.div(blk, 2), 2)
    y = lax.div(inner, 2)

    def at(z, x, y, core):
        return {
            "blk": z * 4 + lax.rem(x, 2) * 2 + core,
            "inner": y * 2 + lax.div(x, 2),
        }

    xs = [at(z, lax.rem(x + k, 4), y, core) for k in range(4)]
    ys = [at(z, x, lax.rem(y + k, 4), core) for k in range(4)]
    zs = [at(lax.rem(z + k, 8), x, y, core) for k in range(8)]
    sib = at(z, x, y, 1 - core)
    near = {"+x": xs[1], "-x": xs[3], "+y": ys[1], "-y": ys[3], "+z": zs[1], "-z": zs[7]}

    barrier = pltpu.get_barrier_semaphore()
    partners = list(near.values()) + [sib]
    for device in partners:
        pl.semaphore_signal(barrier, inc=1, device_id=device, device_id_type=MESH)

    def unit32(ref):
        values = ref[...].astype(jnp.float32)
        norm = jnp.sqrt(jnp.sum(values * values, axis=-1, keepdims=True) + 1e-06)
        return values / norm, norm

    ids = ids_ref[...]
    row = lax.broadcasted_iota(jnp.int32, (16, 128), 0)
    high = jnp.broadcast_to((ids >> 6).astype(jnp.float32), (16, 128))
    low = jnp.broadcast_to((ids & 63).astype(jnp.float32), (16, 128))
    id_rows = jnp.where(row == 0, high, jnp.where(row == 1, low, 0.0)).astype(jnp.bfloat16)
    def place_own(ref, slots):
        unit = unit32(ref)[0].astype(jnp.bfloat16)
        for c in range(TILES):
            slots[pl.ds(c * 128, 128), :] = unit[:, c * 128 : (c + 1) * 128]
        slots[pl.ds(D, 16), :] = id_rows

    place_own(echo_ref, irx)
    pl.semaphore_wait(barrier, len(partners))

    def remote(src, dst, send, recv, device):
        return pltpu.make_async_remote_copy(
            src_ref=src, dst_ref=dst, send_sem=send, recv_sem=recv,
            device_id=device, device_id_type=MESH,
        )

    def img_copy(move):
        k, slot, there, lo, hi, direction = move
        return remote(
            irx.at[pl.ds(slot * BLOCK + lo, hi - lo)], irx.at[pl.ds(there * BLOCK + lo, hi - lo)],
            ig_s.at[k], ig_r.at[k], near[direction],
        )

    def txt_copy(move):
        k, slot, there, lo, hi, direction = move
        return remote(
            trx.at[pl.ds(slot * BLOCK + lo, hi - lo)], trx.at[pl.ds(there * BLOCK + lo, hi - lo)],
            tg_s.at[k], tg_r.at[k], near[direction],
        )

    def sib_copy(k):
        return remote(
            trx.at[pl.ds(k * BLOCK, BLOCK)], trx.at[pl.ds((8 + k) * BLOCK, BLOCK)],
            sg_s.at[k], sg_r.at[k], sib,
        )

    def start(copy, moves):
        for move in moves:
            copy(move).start()

    def arrived(copy, moves):
        for move in moves:
            copy(move).wait_recv()

    def sib_start(*places):
        for dz in places:
            sib_copy(TPLACE[dz]).start()

    def sib_wait(*places):
        for dz in places:
            sib_copy(TPLACE[dz]).wait_recv()

    def ids_of(slots, base):
        pair = slots[pl.ds(base + D, 16), :].astype(jnp.float32)
        return pair[0:1, :] * 64.0 + pair[1:2, :]

    def take_img(first, count):
        def body(s, carry):
            base = pl.multiple_of(s * BLOCK, 16)
            rows = pl.ds(pl.multiple_of(s * 128, 128), 128)
            for c in range(TILES):
                img[rows, c * 128 : (c + 1) * 128] = irx[pl.ds(base + c * 128, 128), :]
            idi[rows, :] = jnp.broadcast_to(ids_of(irx, base), (128, 128)).T
            return carry
        lax.fori_loop(first, first + count, body, 0)

    def take_txt(lane, *places):
        for dz in places:
            k, slot = TPLACE[dz], TSLOT[dz, lane]
            base = (8 * lane + k) * BLOCK
            for c in range(TILES):
                txt[slot * 128 : (slot + 1) * 128, c * 128 : (c + 1) * 128] = trx[
                    pl.ds(base + c * 128, 128), :
                ]
            idt[:, slot * 128 : (slot + 1) * 128] = ids_of(trx, base)

    scale = sharp_ref[0] * (1.0 / math.log(2.0))
    shift = offset_ref[0] * (1.0 / math.log(2.0))

    def pairs(i0, ni, j0, nj):
        rows, cols = pl.ds(i0, ni), pl.ds(j0, nj)
        dots = lax.dot_general(
            img[rows, :], txt[cols, :], (((1,), (1,)), ((), ())),
            preferred_element_type=jnp.float32,
        )
        logits = dots * scale + shift
        match = jnp.concatenate([idi[rows, :]] * (nj // 128), axis=1) == idt[:, cols]
        power = jnp.exp2(jnp.where(match, -logits, logits))
        whole = 1.0 + power
        part = power * pl.reciprocal(whole, approx=True)
        weights = jnp.where(match, -part, part).astype(jnp.bfloat16)
        terms = jnp.log2(whole).reshape(ni // 8, 8, nj).sum(axis=0)
        total[...] += sum(terms[:, c * 128 : (c + 1) * 128] for c in range(nj // 128))
        gi[rows, :] += jnp.dot(weights, txt[cols, :], preferred_element_type=jnp.float32)
        gt[cols, :] += lax.dot_general(
            weights, img[rows, :], (((0,), (0,)), ((), ())),
            preferred_element_type=jnp.float32,
        )

    def summed(acc, block, lo, hi, lands):
        tile, first = lo // 128, lo % 128
        value = acc[
            pl.ds(block * 128 + first, hi - lo), tile * 128 : (tile + 1) * 128
        ]
        for land, base, top, end in lands:
            if top <= lo and hi <= end:
                value = value + land[pl.ds(base + lo - top, hi - lo), :].astype(jnp.float32)
        return value

    def img_lands(slot):
        return [(iland, base, lo, hi) for lo, hi, base in IMG_IN.get(slot, [])]

    def txt_lands(k):
        return [(sland, k * D, 0, D)] + [
            (tland, base, lo, hi) for lo, hi, base in TXT_IN.get(k, [])
        ]

    def pack(acc, block, out, base, lo, hi, lands):
        for first, end in spans(lo, hi):
            out[pl.ds(base + first, end - first), :] = summed(
                acc, block, first, end, lands
            ).astype(jnp.bfloat16)

    def img_back(move):
        k, slot, _, lo, hi, direction, land = move
        return remote(
            isend.at[pl.ds(slot * D + lo, hi - lo)], iland.at[pl.ds(land, hi - lo)],
            is_s.at[k], is_r.at[k], near[direction],
        )

    def txt_back(move):
        k, slot, _, lo, hi, direction, land = move
        return remote(
            tsend.at[pl.ds(slot * D + lo, hi - lo)], tland.at[pl.ds(land, hi - lo)],
            ts_s.at[k], ts_r.at[k], near[direction],
        )

    def sib_back(k):
        return remote(
            ssend.at[pl.ds(k * D, D)], sland.at[pl.ds(k * D, D)], ss_s.at[k], ss_r.at[k], sib
        )

    def img_give(moves):
        for move in moves:
            _, slot, _, lo, hi, _, _ = move
            pack(gi, slot, isend, slot * D, lo, hi, img_lands(slot))
            img_back(move).start()

    def sib_give(*places):
        for dz in places:
            k = TPLACE[dz]
            pack(gt, TSLOT[dz, 1], ssend, k * D, 0, D, [])
            sib_back(k).start()

    def sib_got(*places):
        for dz in places:
            sib_back(TPLACE[dz]).wait_recv()

    def txt_give(moves):
        for move in moves:
            _, k, _, lo, hi, _, _ = move
            pack(gt, TSLOT[DZ[k], 0], tsend, k * D, lo, hi, txt_lands(k))
            txt_back(move).start()

    def loss_copies(step):
        buf, me, devices, first = (
            (lc, core, [sib], 0), (lx, x, xs[1:], 1), (ly, y, ys[1:], 4), (lz, z, zs[1:], 7)
        )[step]
        copies = [
            remote(buf.at[me], buf.at[me], l_s.at[first + k], l_r.at[first + k], device)
            for k, device in enumerate(devices)
        ]
        return buf, me, copies

    def loss_give(step, value):
        buf, me, copies = loss_copies(step)
        buf[me] = value
        for copy in copies:
            copy.start()

    def loss_take(step):
        buf, _, copies = loss_copies(step)
        for copy in copies:
            copy.wait_recv()
        return sum(buf[k] for k in range(buf.shape[0]))

    I, T, IB, TB = IMG_OUT, TXT_OUT, IMG_BACK, TXT_BACK
    start(img_copy, I[0][:4])
    place_own(footage_ref, trx)
    start(txt_copy, T[0][:2])
    start(img_copy, I[0][4:])
    start(txt_copy, T[0][2:])
    sib_start(0)
    gi[...] = jnp.zeros_like(gi)
    gt[...] = jnp.zeros_like(gt)
    total[...] = jnp.zeros_like(total)
    take_img(0, 1)
    take_txt(0, 0)

    arrived(img_copy, I[0][:4])
    start(img_copy, I[1])
    arrived(txt_copy, T[0][:2])
    start(txt_copy, T[1])
    sib_wait(0)
    take_txt(1, 0)

    arrived(img_copy, I[0][4:])
    start(img_copy, I[2])
    arrived(txt_copy, T[0][2:])
    start(txt_copy, T[2])
    sib_start(1, 7)
    take_img(1, 4)
    take_txt(0, 1, 7)
    pairs(0, 640, 0, 512)

    arrived(img_copy, I[1][:4])
    start(img_copy, I[3])
    arrived(txt_copy, T[1])
    start(txt_copy, T[3])
    sib_wait(1, 7)
    take_txt(1, 1, 7)
    pairs(0, 640, 512, 256)

    arrived(img_copy, I[1][4:])
    start(img_copy, I[4])
    arrived(txt_copy, T[2])
    start(txt_copy, T[4])
    sib_start(2, 6)
    take_txt(0, 2, 6)
    pairs(0, 640, 768, 256)

    arrived(img_copy, I[2])
    start(img_copy, I[5])
    arrived(txt_copy, T[3])
    start(txt_copy, T[5])
    take_img(5, 6)
    pairs(640, 768, 0, 512)

    arrived(img_copy, I[3][:4])
    start(img_copy, I[6])
    arrived(txt_copy, T[4])
    sib_start(3, 5)
    sib_wait(2, 6)
    take_txt(1, 2, 6)
    pairs(640, 768, 512, 512)

    arrived(txt_copy, T[5])
    sib_start(4)
    pairs(0, 1408, 1024, 256)

    for moves in (I[3][4:], I[4], I[5], I[6]):
        arrived(img_copy, moves)
    take_img(11, 5)
    pairs(1408, 640, 0, 1280)
    take_txt(0, 3, 5, 4)
    sib_wait(3, 5, 4)
    take_txt(1, 3, 5, 4)
    sib_give(2, 6, 1, 7, 0)
    pairs(1408, 640, 1280, 768)
    img_give(IB[6])
    for moves in (IB[5], IB[4], IB[3][4:]):
        img_give(moves)
    pairs(0, 1408, 1792, 256)
    sib_give(4)
    sib_got(2, 6, 1, 7, 0)
    pairs(640, 768, 1280, 512)
    arrived(img_back, IB[6])
    img_give(IB[3][:4])
    for moves in (IB[5], IB[4], IB[3][4:]):
        arrived(img_back, moves)
    first = [IB[1][1], IB[2][2], IB[2][3], IB[1][2], IB[2][4], IB[1][4], IB[1][5], IB[2][5]]
    third = [IB[2][0], IB[2][1]]
    late = [IB[1][0], IB[1][3]]
    img_give(first)
    img_give(third)
    sib_got(4)
    txt_give(TB[5])
    pairs(0, 640, 1280, 512)

    sib_give(3, 5)
    loss_give(0, total[...])
    home = {(slot, lo): move for move in IB[0] for _, slot, _, lo, _, _, _ in [move]}
    arrived(img_back, IB[3][:4])
    img_give(late)
    img_give([home[2, 384], home[3, 0]])
    sib_got(3, 5)
    txt_give(TB[4])
    arrived(txt_back, TB[5])
    txt_give(TB[3])
    loss_give(1, loss_take(0))
    arrived(img_back, first)
    img_give([home[1, 0], home[4, 384]])
    arrived(txt_back, TB[4])
    txt_give(TB[2])
    loss_give(2, loss_take(1))
    arrived(img_back, third)
    img_give([home[1, 384], home[4, 0]])
    arrived(txt_back, TB[3])
    txt_give(TB[1])
    arrived(img_back, late)
    img_give([home[2, 0], home[3, 384]])
    loss_give(3, loss_take(2))
    arrived(txt_back, TB[2])
    txt_give(TB[0][2:])
    arrived(txt_back, TB[1])
    txt_give(TB[0][:2])
    loss_ref[...] = jnp.broadcast_to(
        jnp.sum(loss_take(3), keepdims=True) * (math.log(2.0) / BATCH), (8, 128)
    )

    def finish(ref, acc, lands, out):
        unit, norm = unit32(ref)
        tiles = [summed(acc, 0, c * 128, (c + 1) * 128, lands) for c in range(TILES)]
        grad = jnp.concatenate(tiles, axis=1) * sharp_ref[0]
        along = jnp.sum(unit * grad, axis=-1, keepdims=True)
        out[...] = ((grad - unit * along) / norm).astype(jnp.bfloat16)

    arrived(img_back, IB[0])
    finish(echo_ref, gi, img_lands(0), gimg_ref)
    arrived(txt_back, TB[0])
    finish(footage_ref, gt, txt_lands(0), gtxt_ref)

    for moves in I:
        for move in moves:
            img_copy(move).wait_send()
    for moves in T:
        for move in moves:
            txt_copy(move).wait_send()
    for moves in IB:
        for move in moves:
            img_back(move).wait_send()
    for moves in TB:
        for move in moves:
            txt_back(move).wait_send()
    for r in range(4):
        for copy in loss_copies(r)[2]:
            copy.wait_send()
    for k in range(8):
        sib_copy(k).wait_send()
        sib_back(k).wait_send()


def per_device(echo_vectors, footage_vectors, match_numbers, sharpness_factor, score_offset):
    bf16, f32 = jnp.bfloat16, jnp.float32
    vmem = pl.BlockSpec(memory_space=pltpu.VMEM)
    smem = pl.BlockSpec(memory_space=pltpu.SMEM)
    dma = pltpu.SemaphoreType.DMA
    grad_image, grad_text, loss = pl.pallas_call(
        kernel,
        name="contrastive_step",
        out_shape=[
            jax.ShapeDtypeStruct((ROWS, D), bf16),
            jax.ShapeDtypeStruct((ROWS, D), bf16),
            jax.ShapeDtypeStruct((8, 128), f32),
        ],
        in_specs=[vmem, vmem, vmem, smem, smem],
        out_specs=[vmem, vmem, vmem],
        scratch_shapes=[
            pltpu.VMEM((SLOTS * BLOCK, 128), bf16),
            pltpu.VMEM((SLOTS * BLOCK, 128), bf16),
            pltpu.VMEM((N, D), bf16),
            pltpu.VMEM((N, D), bf16),
            pltpu.VMEM((N, 128), f32),
            pltpu.VMEM((1, N), f32),
            pltpu.VMEM((N, D), f32),
            pltpu.VMEM((N, D), f32),
            pltpu.VMEM((SLOTS * D, 128), bf16),
            pltpu.VMEM((IMG_LAND, 128), bf16),
            pltpu.VMEM((8 * D, 128), bf16),
            pltpu.VMEM((TXT_LAND, 128), bf16),
            pltpu.VMEM((8 * D, 128), bf16),
            pltpu.VMEM((8 * D, 128), bf16),
            pltpu.VMEM((8, 128), f32),
            pltpu.VMEM((2, 8, 128), f32),
            pltpu.VMEM((4, 8, 128), f32),
            pltpu.VMEM((4, 8, 128), f32),
            pltpu.VMEM((8, 8, 128), f32),
            dma((IMG_N,)), dma((IMG_N,)),
            dma((TXT_N,)), dma((TXT_N,)),
            dma((8,)), dma((8,)),
            dma((IMG_N,)), dma((IMG_N,)),
            dma((TXT_N,)), dma((TXT_N,)),
            dma((8,)), dma((8,)),
            dma((14,)), dma((14,)),
        ],
        compiler_params=pltpu.CompilerParams(
            collective_id=0, has_side_effects=True, vmem_limit_bytes=60 << 20
        ),
    )(echo_vectors, footage_vectors, match_numbers.reshape(1, ROWS), sharpness_factor, score_offset)
    return grad_image, grad_text, loss[0, :1]


def solution(mesh):
    return jax.shard_map(
        per_device,
        mesh=mesh,
        in_specs=(
            P(("blk", "inner"), None),
            P(("blk", "inner"), None),
            P(("blk", "inner")),
            P(),
            P(),
        ),
        out_specs=(P(("blk", "inner"), None), P(("blk", "inner"), None), P()),
        check_vma=False,
    )
```
